256 devices in a mesh: rep: 32 (over x, z), own: 8 (over y, core).
Axes of the slice: x: 4, y: 4, z: 8, core: 2. Of those that a mesh axis runs over, the one named last changes fastest.
Arguments:
- grads: bfloat16 [32, 4096, 4096], P('rep', 'own'), may hold values from -1.1953125 to 1.1953125
- momentum: bfloat16 [8, 512, 8, 512], P(None, 'rep', 'own'), may hold values from -3 to 3
- second: float32 [8, 512, 8, 512], P(None, 'rep', 'own'), may hold values from 0.005 to 200
- left_roots: bfloat16 [8, 8, 512, 512], P(None, 'own', 'rep'), may hold values from -0.10606602 to 2, as said below
- right_roots: bfloat16 [8, 8, 512, 512], P(None, 'own'), may hold values from -0.10606602 to 2, as said below
Outputs:
- direction: bfloat16 [4096, 4096], P('own')
- new_momentum: bfloat16 [8, 512, 8, 512], P(None, 'rep', 'own')
- new_second: float32 [8, 512, 8, 512], P(None, 'rep', 'own')
The draws below stay inside these ranges and needn't reach their ends.
Inputs may be any that keep to these rules, and one draw needn't show every extreme that they name: `left_roots`: each block is symmetric. `right_roots`: each block is symmetric.
All inputs are finite; a program needn't handle non-finite values.
Results may differ from the reference program's by a relative error of at most 0.024.
Values may be sent and summed in bfloat16 or wider, within the bound.
No kernel may reach another device: no remote copies, remote signals or barrier semaphores. Data moves between devices by JAX's collectives and lax.ppermute only.
A program may use at most 128 MiB of HBM per device.

```python
import jax
import jax.numpy as jnp
from jax import lax

D = 4096
BS = 512
NB = 8
REPLICAS = 32


def log_uniform(key, shape, low, high):
    return jnp.exp(jax.random.uniform(key, shape, jnp.float32, jnp.log(low), jnp.log(high)))


def symmetric_blocks(key):
    first, second_key = jax.random.split(key)
    noise = jnp.clip(jax.random.normal(first, (NB, NB, BS, BS), jnp.float32), -4.0, 4.0)
    off_diag = (noise + jnp.swapaxes(noise, 2, 3)) * (0.3 / BS ** 0.5)
    eye_mask = jnp.eye(BS, dtype=jnp.float32)
    diag_vals = jax.random.uniform(second_key, (NB, NB, BS, 1), jnp.float32, 1.0, 2.0)
    return off_diag * (1.0 - eye_mask) + eye_mask * diag_vals


def draw_second(key, part):
    key = jax.random.fold_in(key, 7)
    row_key, col_key, core_key = jax.random.split(key, 3)
    low, high = (0.3, 3.0)
    row_scale = log_uniform(row_key, (NB, BS, 1, 1), low, high)
    col_scale = log_uniform(col_key, (1, 1, NB, BS), low, high)
    core = log_uniform(core_key, (NB, BS, NB, BS), 0.5, 2.0)
    return row_scale * col_scale * core


def draw_left_roots(key, part):
    key = jax.random.fold_in(key, 11)
    return symmetric_blocks(key).astype(jnp.bfloat16)


def draw_right_roots(key, part):
    key = jax.random.fold_in(key, 13)
    return symmetric_blocks(key).astype(jnp.bfloat16)


def spiked(result, rng, source, target, shards_of, factor):
    owner, partner = [(jnp.arange(result.shape[axis_at]) // (result.shape[axis_at] // shards_of)).reshape([-1 if axis == axis_at else 1 for axis in range(result.ndim)]) for axis_at in (source, target)]
    chosen = jax.random.permutation(rng, shards_of)[partner]
    strong = (owner == chosen) | (owner == (partner + shards_of // 2) % shards_of)
    return jnp.where(strong, factor * result, result)


def level_of(rng, extent, cuts, least, top_value):
    factor_of = 1.0
    for axis_at, parts in cuts:
        heights = jax.random.uniform(jax.random.fold_in(jax.random.fold_in(rng, 6), axis_at), (parts,), jnp.float32, least / len(cuts), top_value / len(cuts))
        factor_of = factor_of * jnp.repeat(jnp.exp(heights), extent[axis_at] // parts).reshape((-1,) + (1,) * (len(extent) - 1 - axis_at))
    return factor_of


def centred(own_key, extent, width, most, pieces=(), kind=jnp.bfloat16):
    entries = width * jax.random.normal(own_key, extent, jnp.float32)
    if pieces:
        entries = entries * level_of(own_key, extent, pieces, -0.22, 0.18)
    return jnp.clip(entries, -most, most).astype(kind)


def gaussian_with(stream_key, extent, width, reach, shards, heavy, held_as=jnp.bfloat16):
    values = width * jax.random.normal(stream_key, extent, jnp.float32)
    if shards:
        values = values * level_of(stream_key, extent, shards, -0.22, 0.18)
    return jnp.clip(spiked(values, jax.random.fold_in(stream_key, 3), *heavy), -reach, reach).astype(held_as)


def setup_inputs(seed: int = 0) -> dict:
    streams_of = jax.random.split(jax.random.key(seed), 6)
    grads = gaussian_with(streams_of[0], (REPLICAS, D, D), 0.2, 1.1953125, ((0, 32), (1, 8)), (0, 1, 32, 2.75))
    momentum = centred(streams_of[1], (NB, BS, NB, BS), 0.5, 3.0, ((1, 32), (2, 8)))
    second = draw_second(jax.random.fold_in(streams_of[5], 71), 0)
    left_roots = draw_left_roots(jax.random.fold_in(streams_of[5], 71), 0)
    right_roots = draw_right_roots(jax.random.fold_in(streams_of[5], 71), 0)
    return {"grads": grads, "momentum": momentum, "second": second, "left_roots": left_roots, "right_roots": right_roots}


BETA_ONE = 0.9
BETA_TWO = 0.95
CORRECT_ONE = 1.0 - 0.9 ** 10
CORRECT_TWO = 1.0 - 0.95 ** 10
ADAM_EPS = 1e-08
NORM_EPS = 1e-06

def reference(grads, momentum, second, left_roots, right_roots):
    total = lax.optimization_barrier(jnp.sum(grads, axis=0, dtype=jnp.float32))
    gradient = total.reshape(NB, BS, NB, BS)
    moment_f = BETA_ONE * momentum.astype(jnp.float32) + (1.0 - BETA_ONE) * gradient
    new_second = BETA_TWO * second + (1.0 - BETA_TWO) * gradient * gradient
    adam_step = moment_f / CORRECT_ONE / (jnp.sqrt(new_second / CORRECT_TWO) + ADAM_EPS)
    g_low = lax.optimization_barrier(gradient.astype(jnp.bfloat16)).astype(jnp.float32)
    right_product = jnp.einsum('ikjl,ijlm->ikjm', g_low, right_roots.astype(jnp.float32))
    right_low = lax.optimization_barrier(right_product.astype(jnp.bfloat16)).astype(jnp.float32)
    shampoo = jnp.einsum('ijkl,iljm->ikjm', left_roots.astype(jnp.float32), right_low)
    adam_sq = lax.optimization_barrier(jnp.sum(adam_step * adam_step, axis=(1, 3)))
    shampoo_sq = lax.optimization_barrier(jnp.sum(shampoo * shampoo, axis=(1, 3)))
    graft_scale = jnp.sqrt((adam_sq + NORM_EPS) / (shampoo_sq + NORM_EPS))
    direction = (shampoo * graft_scale[:, None, :, None]).astype(jnp.bfloat16).reshape(D, D)
    return (direction, moment_f.astype(jnp.bfloat16), new_second)
```

```python
import functools

import jax
import jax.numpy as jnp
from jax import lax
from jax.experimental import pallas as pl
from jax.experimental.pallas import tpu as pltpu
from jax.sharding import Mesh, PartitionSpec as P

BETA_ONE = 0.9
BETA_TWO = 0.95
CORRECT_ONE = 1.0 - 0.9**10
CORRECT_TWO = 1.0 - 0.95**10
ADAM_EPS = 1e-08
NORM_EPS = 1e-06

NX, NZ, NY, NC = 4, 8, 4, 2
OWN = ("y", "core")
BS = 512
QROWS = BS // NX
DROWS = QROWS // NZ
HROWS = BS // 2
SHIFTS = (0, 1, 3, 2)
SUMS = 16
HALF = NZ * BS // 2
VMEM = 40 * 1024 * 1024
PARAMS = pltpu.CompilerParams(vmem_limit_bytes=VMEM)
ALL_VMEM = pltpu.CompilerParams(vmem_limit_bytes=57 * 1024 * 1024)
F32, BF16 = jnp.float32, jnp.bfloat16


def cost(flops, nbytes):
    return pl.CostEstimate(flops=flops, bytes_accessed=nbytes, transcendentals=0)


def moments(g, m, v):
    moment = BETA_ONE * m.astype(F32) + (1.0 - BETA_ONE) * g
    second = BETA_TWO * v.astype(F32) + (1.0 - BETA_TWO) * g * g
    return moment, second


def staged(loads, stores, sems):
    for k, (src, dst) in enumerate(loads):
        pltpu.make_async_copy(src, dst, sems.at[0, k]).start()
    for k, (src, dst) in enumerate(loads):
        pltpu.make_async_copy(src, dst, sems.at[0, k]).wait()
        if k < len(stores):
            pltpu.make_async_copy(*stores[k], sems.at[1, k]).start()
    for k, (src, dst) in enumerate(stores):
        pltpu.make_async_copy(src, dst, sems.at[1, k]).wait()


def pick_kernel(x_ref, src_ref, left_ref, right_ref, hold_ref, sems):
    loads, stores = [], []
    for half, out_ref in enumerate((left_ref, right_ref)):
        for k, bits in enumerate(((1, 2), (3, 2))[half]):
            cols = pl.ds(half * HALF, HALF)
            held = hold_ref.at[2 * half + k]
            loads.append((src_ref.at[x_ref[0] ^ bits, :, cols], held))
            stores.append((held, out_ref.at[k]))
    staged(loads, stores, sems)


def pick(grads, x):
    anywhere = pl.BlockSpec(memory_space=pl.ANY)
    return pl.pallas_call(
        pick_kernel,
        in_specs=[pl.BlockSpec(memory_space=pltpu.SMEM), anywhere],
        out_specs=(anywhere, anywhere),
        out_shape=(jax.ShapeDtypeStruct((2, QROWS, HALF), BF16),) * 2,
        scratch_shapes=[pltpu.VMEM((4, QROWS, HALF), BF16), pltpu.SemaphoreType.DMA((2, 4))],
        compiler_params=ALL_VMEM,
        cost_estimate=cost(0, 4 << 20),
    )(x, grads)


def pack_kernel(x_ref, z_ref, after_ref, right_ref, *refs):
    out_ref, hold_ref, sems = refs[-3:]
    row = pl.multiple_of(x_ref[0] * QROWS + z_ref[0] * DROWS, DROWS)
    parts = [right_ref.at[:, pl.ds(row, DROWS)], *refs[:-3]]
    loads = [
        (part, hold_ref.at[:, pl.ds(k * DROWS, DROWS)]) for k, part in enumerate(parts)
    ]
    staged(loads[:-1], [], sems)
    staged(loads[-1:], [(hold_ref, out_ref)], sems)


def pack(x, z, after, right, *states):
    anywhere = pl.BlockSpec(memory_space=pl.ANY)
    smem = pl.BlockSpec(memory_space=pltpu.SMEM)
    shape = (NZ, (1 + len(states)) * DROWS, BS)
    return pl.pallas_call(
        pack_kernel,
        in_specs=[smem, smem] + [anywhere] * (2 + len(states)),
        out_specs=anywhere,
        out_shape=jax.ShapeDtypeStruct(shape, BF16),
        scratch_shapes=[pltpu.VMEM(shape, BF16), pltpu.SemaphoreType.DMA((2, 4))],
        compiler_params=ALL_VMEM,
        cost_estimate=cost(0, 1 << 20),
    )(x, z, after, right, *states)


def add_kernel(where_ref, src_ref, got_ref, out_ref):
    out_ref[...] = (src_ref[0].astype(F32) + got_ref[0].astype(F32)).astype(BF16)


def add_quarter(grads, got, quarter, half):
    return pl.pallas_call(
        add_kernel,
        grid_spec=pltpu.PrefetchScalarGridSpec(
            num_scalar_prefetch=1,
            grid=(2,),
            in_specs=[
                pl.BlockSpec((1, QROWS, HALF // 2), lambda c, where: (where[0], 0, 2 * half + c)),
                pl.BlockSpec((1, QROWS, HALF // 2), lambda c, where: (1, 0, c)),
            ],
            out_specs=pl.BlockSpec((QROWS, HALF // 2), lambda c, where: (0, c)),
        ),
        out_shape=jax.ShapeDtypeStruct((QROWS, HALF), BF16),
        compiler_params=PARAMS,
        cost_estimate=cost(1 << 19, 3 << 19),
    )(quarter, grads, got)


def sum_kernel(where_ref, *refs):
    out_ref = refs[-1]
    for half in range(2):
        mine_ref, first_ref, second_ref = refs[3 * half : 3 * half + 3]
        total = mine_ref[0].astype(F32) + first_ref[0].astype(F32) + second_ref[...].astype(F32)
        out_ref[half, 0] = total.astype(BF16)


def sum_quarter(grads, firsts, seconds, quarter):
    specs, args = [], []
    for half in range(2):
        specs += [
            pl.BlockSpec((1, QROWS, BS), lambda j, where, half=half: (where[0], 0, 4 * half + j)),
            pl.BlockSpec((1, QROWS, BS), lambda j, where: (0, 0, j)),
            pl.BlockSpec((QROWS, BS), lambda j, where: (0, j)),
        ]
        args += [grads, firsts[half], seconds[half]]
    total = pl.pallas_call(
        sum_kernel,
        grid_spec=pltpu.PrefetchScalarGridSpec(
            num_scalar_prefetch=1,
            grid=(NZ // 2,),
            in_specs=specs,
            out_specs=pl.BlockSpec((2, 1, QROWS, BS), lambda j, where: (0, j, 0, 0)),
        ),
        out_shape=jax.ShapeDtypeStruct((2, NZ // 2, QROWS, BS), BF16),
        compiler_params=PARAMS,
        cost_estimate=cost(1 << 20, 28 << 20),
    )(quarter, *args)
    return total.reshape(NZ, QROWS, BS)


def right_kernel(x_ref, parts_ref, pre_ref, *refs):
    roots, (low_ref, prod_ref) = refs[:NX], refs[NX:]
    g = parts_ref[0].astype(F32)
    for k in range(1, NZ):
        g += parts_ref[k].astype(F32)
    low_ref[...] = g.astype(BF16)
    prod = None
    for by, root_ref in zip(SHIFTS, roots):
        col = pl.multiple_of(lax.rem(x_ref[0] + NX - by, NX) * QROWS, QROWS)
        right = root_ref[:, :DROWS].reshape(QROWS, BS)
        term = jnp.dot(low_ref[:, pl.ds(col, QROWS)], right, preferred_element_type=F32)
        prod = term if prod is None else prod + term
    prod_ref[:QROWS] = prod.astype(BF16)
    m = pre_ref[:, 2 * DROWS : 3 * DROWS].reshape(QROWS, BS)
    v = pre_ref[:, 3 * DROWS :].reshape(QROWS, BS)
    moment, second = moments(g, m, v)
    step = moment / CORRECT_ONE / (jnp.sqrt(second / CORRECT_TWO) + ADAM_EPS)
    total = jnp.full((SUMS, BS), jnp.sum(step * step), F32)
    high = total.astype(BF16).astype(F32)
    first = lax.broadcasted_iota(jnp.int32, (SUMS, BS), 0) == 0
    prod_ref[QROWS:] = jnp.where(first, high, total - high).astype(BF16)


def right_stage(x, parts, pre, roots):
    full = pl.BlockSpec(memory_space=pltpu.VMEM)
    return pl.pallas_call(
        right_kernel,
        in_specs=[pl.BlockSpec(memory_space=pltpu.SMEM)] + [full] * (2 + NX),
        out_shape=(
            jax.ShapeDtypeStruct((QROWS, BS), BF16),
            jax.ShapeDtypeStruct((QROWS + SUMS, BS), BF16),
        ),
        compiler_params=PARAMS,
        cost_estimate=cost(1 << 26, 2 << 20),
    )(x, parts, pre, *roots)


def left_kernel(x_ref, *refs):
    prods, roots, (out_ref, up_ref, down_ref) = refs[:NX], refs[NX : 2 * NX], refs[2 * NX :]
    shampoo, adam_sq = None, None
    for prod_ref, root_ref in zip(prods, roots):
        term = lax.dot_general(
            root_ref[:, DROWS:].reshape(QROWS, BS),
            prod_ref[:QROWS],
            (((0,), (0,)), ((), ())),
            preferred_element_type=F32,
        )
        sums = prod_ref[QROWS:].astype(F32)
        part = sums[0:1, 0:1] + sums[1:2, 0:1]
        shampoo = term if shampoo is None else shampoo + term
        adam_sq = part if adam_sq is None else adam_sq + part
    scale = jnp.sqrt((adam_sq + NORM_EPS) / (jnp.sum(shampoo * shampoo) + NORM_EPS))
    out_ref[...] = (shampoo * scale).astype(BF16)
    up_ref[...] = out_ref[pl.ds(pl.multiple_of((x_ref[0] & 1) * HROWS, HROWS), HROWS)]
    down_ref[...] = out_ref[pl.ds(pl.multiple_of((x_ref[0] >> 1) * HROWS, HROWS), HROWS)]


def left_stage(x, prods, roots):
    full = pl.BlockSpec(memory_space=pltpu.VMEM)
    return pl.pallas_call(
        left_kernel,
        in_specs=[pl.BlockSpec(memory_space=pltpu.SMEM)] + [full] * (2 * NX),
        out_shape=(
            jax.ShapeDtypeStruct((BS, BS), BF16),
            jax.ShapeDtypeStruct((HROWS, BS), BF16),
            jax.ShapeDtypeStruct((HROWS, BS), BF16),
        ),
        compiler_params=PARAMS,
        cost_estimate=cost(1 << 28, 3 << 19),
    )(x, *prods, *roots)


def place_kernel(spots, x_ref, z_ref, *refs):
    srcs, out_ref, sems = refs[:-2], refs[-2], refs[-1]
    halves = {"up": x_ref[0] & 1, "down": x_ref[0] >> 1}
    copies = []
    for k, (src, ring, other, quarter, by) in enumerate(zip(srcs, *zip(*spots))):
        half = 0 if ring is None else (1 - halves[ring] if other else halves[ring])
        row = pl.multiple_of(half * HROWS + quarter * QROWS, QROWS)
        col = pl.multiple_of(lax.rem(z_ref[0] + by, NZ) * BS, BS)
        dst = out_ref.at[pl.ds(row, src.shape[0]), pl.ds(col, BS)]
        copies.append(pltpu.make_async_copy(src, dst, sems.at[k]))
        copies[-1].start()
    for copy in copies:
        copy.wait()


def place(x, z, pieces):
    srcs, spots = [piece[0] for piece in pieces], [piece[1:] for piece in pieces]
    anywhere = pl.BlockSpec(memory_space=pl.ANY)
    smem = pl.BlockSpec(memory_space=pltpu.SMEM)
    return pl.pallas_call(
        functools.partial(place_kernel, spots),
        in_specs=[smem, smem] + [pl.BlockSpec(memory_space=pltpu.VMEM)] * len(srcs),
        out_specs=anywhere,
        out_shape=jax.ShapeDtypeStruct((BS, NZ * BS), BF16),
        scratch_shapes=[pltpu.SemaphoreType.DMA((len(pieces),))],
        compiler_params=PARAMS,
        cost_estimate=cost(0, 4 * sum(src.size for src in srcs)),
    )(x, z, *srcs)


def shift(value, axis, size, by):
    return lax.ppermute(value, axis, [(k, (k + by) % size) for k in range(size)])


def partner(value, bits):
    return lax.ppermute(value, "x", [(k, k ^ bits) for k in range(NX)])


def swap_z_own(value):
    pairs = [(i * NZ + j, j * NZ + i) for i in range(NZ) for j in range(NZ)]
    return lax.ppermute(value, ("z", *OWN), pairs)


def gather_x(value):
    return [value] + [shift(value, "x", NX, by) for by in SHIFTS[1:]]


def exchange(value, axis):
    return lax.all_to_all(value, axis, split_axis=0, concat_axis=0, tiled=True)


def after(value, *others):
    return lax.optimization_barrier((value, *others))[0]


def on_device(grads, momentum, second, left_roots, right_roots):
    x, z = lax.axis_index("x").reshape(1), lax.axis_index("z").reshape(1)
    quarters = grads[0].reshape(NX, QROWS, grads.shape[2])

    steps = (1, 3)
    sends = pick(quarters, x)
    firsts = [partner(sends[h], steps[h]) for h in range(2)]

    low_second = after(second, sends[1])[:, :, 0].astype(BF16)
    pre = pack(
        x, z, sends[1], right_roots[:, 0], left_roots[:, 0], momentum[:, :, 0], low_second
    )
    pre = exchange(after(exchange(pre, OWN), *firsts), "z")
    roots = gather_x(pre[:, : 2 * DROWS])

    seconds = [
        partner(add_quarter(quarters, firsts[h], x ^ steps[1 - h], h), steps[1 - h])
        for h in range(2)
    ]
    over_z = exchange(sum_quarter(quarters, firsts, seconds, x), "z")
    g_low, prod = right_stage(x, over_z, pre, roots)
    block, up, down = left_stage(x, gather_x(prod), roots)

    pieces = [(block, None, False, 0, 0)]
    g_state = swap_z_own(g_low)
    waits, last = (), (g_state,)
    for step in range(1, NZ // 2):
        up, down = (after(half, *waits) for half in (up, down))
        up, down = shift(up, "z", NZ, 1), shift(down, "z", NZ, NZ - 1)
        others = [partner(up, 1), partner(down, 3)]
        pieces += [
            (up, "up", False, 0, NZ - step),
            (down, "down", False, 0, step),
            (others[0], "up", True, 0, NZ - step),
            (others[1], "down", True, 0, step),
        ]
        waits, last = last, others
    up, down = (after(half, *waits) for half in (up, down))
    up, down = shift(up[:QROWS], "z", NZ, 1), shift(down[QROWS:], "z", NZ, NZ - 1)
    pieces += [
        (up, "up", False, 0, NZ // 2),
        (down, "down", False, 1, NZ // 2),
        (partner(up, 1), "up", True, 0, NZ // 2),
        (partner(down, 3), "down", True, 1, NZ // 2),
    ]

    g = exchange(after(g_state, *waits).reshape(NZ, DROWS, BS), "z").astype(F32)[:, :, None]
    new_moment, new_second = moments(g, momentum, second)
    return place(x, z, pieces), new_moment.astype(BF16), new_second


def solution(mesh):
    named = Mesh(mesh.devices.reshape(NX, NZ, NY, NC), ("x", "z", "y", "core"))
    rep = ("x", "z")
    in_specs = (
        P(rep, OWN, None),
        P(None, rep, OWN, None),
        P(None, rep, OWN, None),
        P(None, OWN, rep, None),
        P(None, OWN, None, None),
    )
    out_specs = (P(OWN, None), P(None, rep, OWN, None), P(None, rep, OWN, None))
    return jax.shard_map(
        on_device, mesh=named, in_specs=in_specs, out_specs=out_specs, check_vma=False
    )
```

```python
import functools

import jax
import jax.numpy as jnp
from jax import lax
from jax.experimental import pallas as pl
from jax.experimental.pallas import tpu as pltpu
from jax.sharding import Mesh, PartitionSpec as P

BETA_ONE = 0.9
BETA_TWO = 0.95
CORRECT_ONE = 1.0 - 0.9**10
CORRECT_TWO = 1.0 - 0.95**10
ADAM_EPS = 1e-08
NORM_EPS = 1e-06

NX, NZ, NY, NC = 4, 8, 4, 2
OWN = ("y", "core")
BS = 512
QROWS = BS // NX
DROWS = QROWS // NZ
HROWS = BS // 2
SUMS = 16
HALF = NZ * BS // 2
VMEM = 40 * 1024 * 1024
PARAMS = pltpu.CompilerParams(vmem_limit_bytes=VMEM)
ALL_VMEM = pltpu.CompilerParams(vmem_limit_bytes=57 * 1024 * 1024)
F32, BF16 = jnp.float32, jnp.bfloat16


def cost(flops, nbytes):
    return pl.CostEstimate(flops=flops, bytes_accessed=nbytes, transcendentals=0)


def moments(g, m, v):
    moment = BETA_ONE * m.astype(F32) + (1.0 - BETA_ONE) * g
    second = BETA_TWO * v.astype(F32) + (1.0 - BETA_TWO) * g * g
    return moment, second


def staged(loads, stores, sems):
    for k, (src, dst) in enumerate(loads):
        pltpu.make_async_copy(src, dst, sems.at[0, k]).start()
    for k, (src, dst) in enumerate(loads):
        pltpu.make_async_copy(src, dst, sems.at[0, k]).wait()
        if k < len(stores):
            pltpu.make_async_copy(*stores[k], sems.at[1, k]).start()
    for k, (src, dst) in enumerate(stores):
        pltpu.make_async_copy(src, dst, sems.at[1, k]).wait()


def pick_kernel(x_ref, src_ref, left_ref, right_ref, hold_ref, sems):
    loads, stores = [], []
    for half, out_ref in enumerate((left_ref, right_ref)):
        for k, bits in enumerate(((1, 2), (3, 2))[half]):
            cols = pl.ds(half * HALF, HALF)
            held = hold_ref.at[2 * half + k]
            loads.append((src_ref.at[x_ref[0] ^ bits, :, cols], held))
            stores.append((held, out_ref.at[k]))
    staged(loads, stores, sems)


def pick(grads, x):
    anywhere = pl.BlockSpec(memory_space=pl.ANY)
    return pl.pallas_call(
        pick_kernel,
        in_specs=[pl.BlockSpec(memory_space=pltpu.SMEM), anywhere],
        out_specs=(anywhere, anywhere),
        out_shape=(jax.ShapeDtypeStruct((2, QROWS, HALF), BF16),) * 2,
        scratch_shapes=[pltpu.VMEM((4, QROWS, HALF), BF16), pltpu.SemaphoreType.DMA((2, 4))],
        compiler_params=ALL_VMEM,
        cost_estimate=cost(0, 4 << 20),
    )(x, grads)


def pack_kernel(z_ref, own_ref, after_ref, right_ref, *refs):
    states, (out_ref, root_ref, hold_ref, hold_root_ref, sems) = refs[:-5], refs[-5:]
    root = pltpu.make_async_copy(
        right_ref.at[lax.rem(z_ref[0] + NZ - own_ref[0], NZ)], hold_root_ref, sems.at[0, NZ]
    )
    loads = [
        pltpu.make_async_copy(ref, hold_ref.at[:, pl.ds(k * DROWS, DROWS)], sems.at[0, k])
        for k, ref in enumerate(states)
    ]
    for copy in (*loads, root):
        copy.start()
    for copy in loads:
        copy.wait()
    stores = [
        pltpu.make_async_copy(
            hold_ref.at[i], out_ref.at[lax.rem(own_ref[0] + i, NZ)], sems.at[1, i]
        )
        for i in range(NZ)
    ]
    for copy in stores:
        copy.start()
    root.wait()
    stores.append(pltpu.make_async_copy(hold_root_ref, root_ref, sems.at[1, NZ]))
    stores[-1].start()
    for copy in stores:
        copy.wait()


def pack(z, own, after, right, *states):
    anywhere = pl.BlockSpec(memory_space=pl.ANY)
    smem = pl.BlockSpec(memory_space=pltpu.SMEM)
    shape = (NZ, len(states) * DROWS, BS)
    return pl.pallas_call(
        pack_kernel,
        in_specs=[smem, smem] + [anywhere] * (2 + len(states)),
        out_specs=(anywhere, anywhere),
        out_shape=(jax.ShapeDtypeStruct(shape, BF16), jax.ShapeDtypeStruct((BS, BS), BF16)),
        scratch_shapes=[
            pltpu.VMEM(shape, BF16),
            pltpu.VMEM((BS, BS), BF16),
            pltpu.SemaphoreType.DMA((2, NZ + 1)),
        ],
        compiler_params=ALL_VMEM,
        cost_estimate=cost(0, 2 << 20),
    )(z, own, after, right, *states)


def add_kernel(where_ref, src_ref, got_ref, out_ref):
    out_ref[...] = (src_ref[0].astype(F32) + got_ref[0].astype(F32)).astype(BF16)


def add_quarter(grads, got, quarter, half):
    return pl.pallas_call(
        add_kernel,
        grid_spec=pltpu.PrefetchScalarGridSpec(
            num_scalar_prefetch=1,
            grid=(2,),
            in_specs=[
                pl.BlockSpec((1, QROWS, HALF // 2), lambda c, where: (where[0], 0, 2 * half + c)),
                pl.BlockSpec((1, QROWS, HALF // 2), lambda c, where: (1, 0, c)),
            ],
            out_specs=pl.BlockSpec((QROWS, HALF // 2), lambda c, where: (0, c)),
        ),
        out_shape=jax.ShapeDtypeStruct((QROWS, HALF), BF16),
        compiler_params=PARAMS,
        cost_estimate=cost(1 << 19, 3 << 19),
    )(quarter, grads, got)


def sum_kernel(x_ref, own_ref, *refs):
    out_ref, j = refs[-1], pl.program_id(0)
    for half in range(2):
        mine_ref, first_ref, second_ref = refs[3 * half : 3 * half + 3]
        total = mine_ref[0].astype(F32) + first_ref[0].astype(F32) + second_ref[...].astype(F32)
        out_ref[lax.rem(own_ref[0] + half * (NZ // 2) + j, NZ)] = total.astype(BF16)


def sum_quarter(grads, firsts, seconds, x, own):
    specs, args = [], []
    for half in range(2):
        specs += [
            pl.BlockSpec((1, QROWS, BS), lambda j, x, own, half=half: (x[0], 0, 4 * half + j)),
            pl.BlockSpec((1, QROWS, BS), lambda j, x, own: (0, 0, j)),
            pl.BlockSpec((QROWS, BS), lambda j, x, own: (0, j)),
        ]
        args += [grads, firsts[half], seconds[half]]
    return pl.pallas_call(
        sum_kernel,
        grid_spec=pltpu.PrefetchScalarGridSpec(
            num_scalar_prefetch=2,
            grid=(NZ // 2,),
            in_specs=specs,
            out_specs=pl.BlockSpec((NZ, QROWS, BS), lambda j, x, own: (0, 0, 0)),
        ),
        out_shape=jax.ShapeDtypeStruct((NZ, QROWS, BS), BF16),
        compiler_params=PARAMS,
        cost_estimate=cost(1 << 20, 4 << 20),
    )(x, own, *args)


def right_kernel(parts_ref, pre_ref, root_ref, low_ref, prod_ref):
    g = parts_ref[0].astype(F32)
    for k in range(1, NZ):
        g += parts_ref[k].astype(F32)
    low = g.astype(BF16)
    low_ref[...] = low
    prod_ref[:QROWS] = jnp.dot(low, root_ref[...], preferred_element_type=F32).astype(BF16)
    m = pre_ref[:, DROWS : 2 * DROWS].reshape(QROWS, BS)
    v = pre_ref[:, 2 * DROWS :].reshape(QROWS, BS)
    moment, second = moments(g, m, v)
    step = moment / CORRECT_ONE / (jnp.sqrt(second / CORRECT_TWO) + ADAM_EPS)
    total = jnp.full((SUMS, BS), jnp.sum(step * step), F32)
    high = total.astype(BF16).astype(F32)
    first = lax.broadcasted_iota(jnp.int32, (SUMS, BS), 0) == 0
    prod_ref[QROWS:] = jnp.where(first, high, total - high).astype(BF16)


def right_stage(parts, pre, root):
    return pl.pallas_call(
        right_kernel,
        out_shape=(
            jax.ShapeDtypeStruct((QROWS, BS), BF16),
            jax.ShapeDtypeStruct((QROWS + SUMS, BS), BF16),
        ),
        compiler_params=PARAMS,
        cost_estimate=cost(1 << 26, 2 << 20),
    )(parts, pre, root)


def order_kernel(own_ref, src_ref, out_ref):
    for k in range(NZ):
        out_ref[lax.rem(k + NZ - own_ref[0], NZ)] = src_ref[k]


def in_order(own, parts):
    full, smem = pl.BlockSpec(memory_space=pltpu.VMEM), pl.BlockSpec(memory_space=pltpu.SMEM)
    return pl.pallas_call(
        order_kernel,
        in_specs=[smem, full],
        out_specs=full,
        out_shape=jax.ShapeDtypeStruct(parts.shape, BF16),
        compiler_params=PARAMS,
        cost_estimate=cost(0, 1 << 18),
    )(own, parts)


def left_kernel(x_ref, *refs):
    prods, roots, (out_ref, up_ref, down_ref) = refs[:NX], refs[NX : 2 * NX], refs[2 * NX :]
    shampoo, adam_sq = None, None
    for prod_ref, root_ref in zip(prods, roots):
        term = lax.dot_general(
            root_ref[...],
            prod_ref[:QROWS],
            (((0,), (0,)), ((), ())),
            preferred_element_type=F32,
        )
        sums = prod_ref[QROWS:].astype(F32)
        part = sums[0:1, 0:1] + sums[1:2, 0:1]
        shampoo = term if shampoo is None else shampoo + term
        adam_sq = part if adam_sq is None else adam_sq + part
    scale = jnp.sqrt((adam_sq + NORM_EPS) / (jnp.sum(shampoo * shampoo) + NORM_EPS))
    out_ref[...] = (shampoo * scale).astype(BF16)
    up_ref[...] = out_ref[pl.ds(pl.multiple_of((x_ref[0] & 1) * HROWS, HROWS), HROWS)]
    down_ref[...] = out_ref[pl.ds(pl.multiple_of((x_ref[0] >> 1) * HROWS, HROWS), HROWS)]


def left_stage(x, prods, roots):
    full = pl.BlockSpec(memory_space=pltpu.VMEM)
    return pl.pallas_call(
        left_kernel,
        in_specs=[pl.BlockSpec(memory_space=pltpu.SMEM)] + [full] * (2 * NX),
        out_shape=(
            jax.ShapeDtypeStruct((BS, BS), BF16),
            jax.ShapeDtypeStruct((HROWS, BS), BF16),
            jax.ShapeDtypeStruct((HROWS, BS), BF16),
        ),
        compiler_params=PARAMS,
        cost_estimate=cost(1 << 28, 3 << 19),
    )(x, *prods, *roots)


def place_kernel(spots, x_ref, z_ref, own_ref, *refs):
    srcs, out_ref, sems = refs[:-2], refs[-2], refs[-1]
    halves = {"up": x_ref[0] & 1, "down": x_ref[0] >> 1}
    copies = []
    for k, (src, ring, other, quarter, by) in enumerate(zip(srcs, *zip(*spots))):
        half = 0 if ring is None else (1 - halves[ring] if other else halves[ring])
        row = pl.multiple_of(half * HROWS + quarter * QROWS, QROWS)
        col = pl.multiple_of(lax.rem(z_ref[0] + NZ - own_ref[0] + by, NZ) * BS, BS)
        dst = out_ref.at[pl.ds(row, src.shape[0]), pl.ds(col, BS)]
        copies.append(pltpu.make_async_copy(src, dst, sems.at[k]))
        copies[-1].start()
    for copy in copies:
        copy.wait()


def place(x, z, own, pieces):
    srcs, spots = [piece[0] for piece in pieces], [piece[1:] for piece in pieces]
    anywhere = pl.BlockSpec(memory_space=pl.ANY)
    smem = pl.BlockSpec(memory_space=pltpu.SMEM)
    return pl.pallas_call(
        functools.partial(place_kernel, spots),
        in_specs=[smem] * 3 + [pl.BlockSpec(memory_space=pltpu.VMEM)] * len(srcs),
        out_specs=anywhere,
        out_shape=jax.ShapeDtypeStruct((BS, NZ * BS), BF16),
        scratch_shapes=[pltpu.SemaphoreType.DMA((len(pieces),))],
        compiler_params=PARAMS,
        cost_estimate=cost(0, 4 * sum(src.size for src in srcs)),
    )(x, z, own, *srcs)


def shift(value, axis, size, by):
    return lax.ppermute(value, axis, [(k, (k + by) % size) for k in range(size)])


def partner(value, bits):
    return lax.ppermute(value, "x", [(k, k ^ bits) for k in range(NX)])


def mirror(value):
    pairs = [(z * NZ + own, z * NZ + (z - own) % NZ) for z in range(NZ) for own in range(NZ)]
    return lax.ppermute(value, ("z", *OWN), pairs)


def gather_x(value):
    return [value] + [shift(value, "x", NX, by) for by in (1, 3, 2)]


def exchange(value, axis):
    return lax.all_to_all(value, axis, split_axis=0, concat_axis=0, tiled=True)


def after(value, *others):
    return lax.optimization_barrier((value, *others))[0]


def on_device(grads, momentum, second, left_roots, right_roots):
    x, z, own = (lax.axis_index(name).reshape(1) for name in ("x", "z", OWN))
    quarters = grads[0].reshape(NX, QROWS, grads.shape[2])

    steps = (1, 3)
    sends = pick(quarters, x)
    firsts = [partner(sends[h], steps[h]) for h in range(2)]

    low_second = after(second, sends[1])[:, :, 0].astype(BF16)
    pre, root = pack(
        z, own, sends[1], right_roots[:, 0], left_roots[:, 0], momentum[:, :, 0], low_second
    )
    pre = exchange(pre, "z")
    firsts = [after(first, pre) for first in firsts]
    pre, root = mirror(pre), mirror(root)
    roots = gather_x(pre[:, :DROWS].reshape(QROWS, BS))

    seconds = [
        partner(add_quarter(quarters, firsts[h], x ^ steps[1 - h], h), steps[1 - h])
        for h in range(2)
    ]
    over_z = exchange(sum_quarter(quarters, firsts, seconds, x, own), "z")
    g_low, prod = right_stage(over_z, pre, after(root, *roots))
    block, up, down = left_stage(x, gather_x(prod), roots)

    pieces = [(block, None, False, 0, 0)]
    g_state = mirror(g_low)
    waits, last = (), (g_state,)
    for step in range(1, NZ // 2):
        up, down = (after(half, *waits) for half in (up, down))
        up, down = shift(up, "z", NZ, 1), shift(down, "z", NZ, NZ - 1)
        others = [partner(up, 1), partner(down, 3)]
        pieces += [
            (up, "up", False, 0, NZ - step),
            (down, "down", False, 0, step),
            (others[0], "up", True, 0, NZ - step),
            (others[1], "down", True, 0, step),
        ]
        waits, last = last, others
    up, down = (after(half, *waits) for half in (up, down))
    up, down = shift(up[:QROWS], "z", NZ, 1), shift(down[QROWS:], "z", NZ, NZ - 1)
    pieces += [
        (up, "up", False, 0, NZ // 2),
        (down, "down", False, 1, NZ // 2),
        (partner(up, 1), "up", True, 0, NZ // 2),
        (partner(down, 3), "down", True, 1, NZ // 2),
    ]

    g = exchange(after(g_state, *waits).reshape(NZ, DROWS, BS), "z")
    g = in_order(own, g).astype(F32)[:, :, None]
    new_moment, new_second = moments(g, momentum, second)
    return place(x, z, own, pieces), new_moment.astype(BF16), new_second


def solution(mesh):
    named = Mesh(mesh.devices.reshape(NX, NZ, NY, NC), ("x", "z", "y", "core"))
    rep = ("x", "z")
    in_specs = (
        P(rep, OWN, None),
        P(None, rep, OWN, None),
        P(None, rep, OWN, None),
        P(None, OWN, rep, None),
        P(None, OWN, None, None),
    )
    out_specs = (P(OWN, None), P(None, rep, OWN, None), P(None, rep, OWN, None))
    return jax.shard_map(
        on_device, mesh=named, in_specs=in_specs, out_specs=out_specs, check_vma=False
    )
```

```python
import functools

import jax
import jax.numpy as jnp
from jax import lax
from jax.experimental import pallas as pl
from jax.experimental.pallas import tpu as pltpu
from jax.sharding import Mesh, PartitionSpec as P

BETA_ONE = 0.9
BETA_TWO = 0.95
CORRECT_ONE = 1.0 - 0.9**10
CORRECT_TWO = 1.0 - 0.95**10
ADAM_EPS = 1e-08
NORM_EPS = 1e-06

NX, NZ, NY, NC = 4, 8, 4, 2
OWN = ("y", "core")
BS = 512
QROWS = BS // NX
DROWS = QROWS // NZ
HROWS = BS // 2
SUMS = 16
HALF = NZ * BS // 2
VMEM = 40 * 1024 * 1024
PARAMS = pltpu.CompilerParams(vmem_limit_bytes=VMEM)
ALL_VMEM = pltpu.CompilerParams(vmem_limit_bytes=57 * 1024 * 1024)
F32, BF16 = jnp.float32, jnp.bfloat16


def cost(flops, nbytes):
    return pl.CostEstimate(flops=flops, bytes_accessed=nbytes, transcendentals=0)


def moments(g, m, v):
    moment = BETA_ONE * m.astype(F32) + (1.0 - BETA_ONE) * g
    second = BETA_TWO * v.astype(F32) + (1.0 - BETA_TWO) * g * g
    return moment, second


def staged(loads, stores, sems):
    for k, (src, dst) in enumerate(loads):
        pltpu.make_async_copy(src, dst, sems.at[0, k]).start()
    for k, (src, dst) in enumerate(loads):
        pltpu.make_async_copy(src, dst, sems.at[0, k]).wait()
        if k < len(stores):
            pltpu.make_async_copy(*stores[k], sems.at[1, k]).start()
    for k, (src, dst) in enumerate(stores):
        pltpu.make_async_copy(src, dst, sems.at[1, k]).wait()


def pick_kernel(x_ref, src_ref, left_ref, right_ref, hold_ref, sems):
    loads, stores = [], []
    for half, out_ref in enumerate((left_ref, right_ref)):
        for k, bits in enumerate(((1, 2), (3, 2))[half]):
            cols = pl.ds(half * HALF, HALF)
            held = hold_ref.at[2 * half + k]
            loads.append((src_ref.at[x_ref[0] ^ bits, :, cols], held))
            stores.append((held, out_ref.at[k]))
    staged(loads, stores, sems)


def pick(grads, x):
    anywhere = pl.BlockSpec(memory_space=pl.ANY)
    return pl.pallas_call(
        pick_kernel,
        in_specs=[pl.BlockSpec(memory_space=pltpu.SMEM), anywhere],
        out_specs=(anywhere, anywhere),
        out_shape=(jax.ShapeDtypeStruct((2, QROWS, HALF), BF16),) * 2,
        scratch_shapes=[pltpu.VMEM((4, QROWS, HALF), BF16), pltpu.SemaphoreType.DMA((2, 4))],
        compiler_params=ALL_VMEM,
        cost_estimate=cost(0, 4 << 20),
    )(x, grads)


def pack_kernel(x_ref, z_ref, own_ref, after_ref, grads_ref, right_ref, *refs):
    states, (out_ref, root_ref, left_ref, rest_ref) = refs[:-8], refs[-8:-4]
    hold_ref, hold_root_ref, hold_kept_ref, sems = refs[-4:]
    loads = [
        pltpu.make_async_copy(ref, hold_ref.at[:, pl.ds(k * DROWS, DROWS)], sems.at[0, k])
        for k, ref in enumerate(states)
    ]
    stores = [
        pltpu.make_async_copy(
            hold_ref.at[i], out_ref.at[lax.rem(own_ref[0] + i, NZ)], sems.at[1, i]
        )
        for i in range(NZ)
    ]
    root = right_ref.at[lax.rem(z_ref[0] + NZ - own_ref[0], NZ)]
    others = [(root, hold_root_ref, root_ref)]
    for half, bits, kept_ref in ((0, 3, left_ref), (1, 1, rest_ref)):
        src = grads_ref.at[x_ref[0] ^ bits, :, pl.ds(half * HALF, HALF)]
        others.append((src, hold_kept_ref.at[half], kept_ref))
    more = [
        (
            pltpu.make_async_copy(src, hold, sems.at[0, NZ + k]),
            pltpu.make_async_copy(hold, dst, sems.at[1, NZ + k]),
        )
        for k, (src, hold, dst) in enumerate(others)
    ]
    for copy in loads:
        copy.start()
    for load, _ in more:
        load.start()
    for copy in loads:
        copy.wait()
    for copy in stores:
        copy.start()
    for load, store in more:
        load.wait()
        store.start()
    for copy in stores:
        copy.wait()
    for _, store in more:
        store.wait()


def pack(x, z, own, after, grads, right, *states):
    anywhere = pl.BlockSpec(memory_space=pl.ANY)
    smem = pl.BlockSpec(memory_space=pltpu.SMEM)
    shapes = [(NZ, len(states) * DROWS, BS), (BS, BS), (QROWS, HALF), (QROWS, HALF)]
    return pl.pallas_call(
        pack_kernel,
        in_specs=[smem] * 3 + [anywhere] * (3 + len(states)),
        out_specs=(anywhere,) * 4,
        out_shape=tuple(jax.ShapeDtypeStruct(shape, BF16) for shape in shapes),
        scratch_shapes=[
            pltpu.VMEM(shapes[0], BF16),
            pltpu.VMEM(shapes[1], BF16),
            pltpu.VMEM((2, QROWS, HALF), BF16),
            pltpu.SemaphoreType.DMA((2, NZ + 3)),
        ],
        compiler_params=ALL_VMEM,
        cost_estimate=cost(0, 4 << 20),
    )(x, z, own, after, grads, right, *states)


def add_kernel(kept_ref, got_ref, out_ref):
    out_ref[...] = (kept_ref[...].astype(F32) + got_ref[0].astype(F32)).astype(BF16)


def add_quarter(kept, got):
    spec = pl.BlockSpec((QROWS, HALF // 2), lambda c: (0, c))
    return pl.pallas_call(
        add_kernel,
        grid=(2,),
        in_specs=[spec, pl.BlockSpec((1, QROWS, HALF // 2), lambda c: (1, 0, c))],
        out_specs=spec,
        out_shape=jax.ShapeDtypeStruct((QROWS, HALF), BF16),
        compiler_params=PARAMS,
        cost_estimate=cost(1 << 19, 3 << 19),
    )(kept, got)


def sum_kernel(x_ref, own_ref, *refs):
    out_ref, j = refs[-1], pl.program_id(0)
    for half in range(2):
        mine_ref, first_ref, second_ref = refs[3 * half : 3 * half + 3]
        total = mine_ref[0].astype(F32) + first_ref[0].astype(F32) + second_ref[...].astype(F32)
        out_ref[lax.rem(own_ref[0] + half * (NZ // 2) + j, NZ)] = total.astype(BF16)


def sum_quarter(grads, firsts, seconds, x, own):
    specs, args = [], []
    for half in range(2):
        specs += [
            pl.BlockSpec((1, QROWS, BS), lambda j, x, own, half=half: (x[0], 0, 4 * half + j)),
            pl.BlockSpec((1, QROWS, BS), lambda j, x, own: (0, 0, j)),
            pl.BlockSpec((QROWS, BS), lambda j, x, own: (0, j)),
        ]
        args += [grads, firsts[half], seconds[half]]
    return pl.pallas_call(
        sum_kernel,
        grid_spec=pltpu.PrefetchScalarGridSpec(
            num_scalar_prefetch=2,
            grid=(NZ // 2,),
            in_specs=specs,
            out_specs=pl.BlockSpec((NZ, QROWS, BS), lambda j, x, own: (0, 0, 0)),
        ),
        out_shape=jax.ShapeDtypeStruct((NZ, QROWS, BS), BF16),
        compiler_params=PARAMS,
        cost_estimate=cost(1 << 20, 4 << 20),
    )(x, own, *args)


def right_kernel(parts_ref, pre_ref, root_ref, low_ref, prod_ref):
    g = parts_ref[0].astype(F32)
    for k in range(1, NZ):
        g += parts_ref[k].astype(F32)
    low = g.astype(BF16)
    low_ref[...] = low
    prod_ref[:QROWS] = jnp.dot(low, root_ref[...], preferred_element_type=F32).astype(BF16)
    m = pre_ref[:, DROWS : 2 * DROWS].reshape(QROWS, BS)
    v = pre_ref[:, 2 * DROWS :].reshape(QROWS, BS)
    moment, second = moments(g, m, v)
    step = moment / CORRECT_ONE / (jnp.sqrt(second / CORRECT_TWO) + ADAM_EPS)
    total = jnp.full((SUMS, BS), jnp.sum(step * step), F32)
    high = total.astype(BF16).astype(F32)
    first = lax.broadcasted_iota(jnp.int32, (SUMS, BS), 0) == 0
    prod_ref[QROWS:] = jnp.where(first, high, total - high).astype(BF16)


def right_stage(parts, pre, root):
    return pl.pallas_call(
        right_kernel,
        out_shape=(
            jax.ShapeDtypeStruct((QROWS, BS), BF16),
            jax.ShapeDtypeStruct((QROWS + SUMS, BS), BF16),
        ),
        compiler_params=PARAMS,
        cost_estimate=cost(1 << 26, 2 << 20),
    )(parts, pre, root)


def order_kernel(own_ref, src_ref, out_ref):
    for k in range(NZ):
        out_ref[lax.rem(k + NZ - own_ref[0], NZ)] = src_ref[k]


def in_order(own, parts):
    full, smem = pl.BlockSpec(memory_space=pltpu.VMEM), pl.BlockSpec(memory_space=pltpu.SMEM)
    return pl.pallas_call(
        order_kernel,
        in_specs=[smem, full],
        out_specs=full,
        out_shape=jax.ShapeDtypeStruct(parts.shape, BF16),
        compiler_params=PARAMS,
        cost_estimate=cost(0, 1 << 18),
    )(own, parts)


def left_kernel(x_ref, *refs):
    prods, roots, (out_ref, up_ref, down_ref) = refs[:NX], refs[NX : 2 * NX], refs[2 * NX :]
    shampoo, adam_sq = None, None
    for prod_ref, root_ref in zip(prods, roots):
        term = lax.dot_general(
            root_ref[...],
            prod_ref[:QROWS],
            (((0,), (0,)), ((), ())),
            preferred_element_type=F32,
        )
        sums = prod_ref[QROWS:].astype(F32)
        part = sums[0:1, 0:1] + sums[1:2, 0:1]
        shampoo = term if shampoo is None else shampoo + term
        adam_sq = part if adam_sq is None else adam_sq + part
    scale = jnp.sqrt((adam_sq + NORM_EPS) / (jnp.sum(shampoo * shampoo) + NORM_EPS))
    out_ref[...] = (shampoo * scale).astype(BF16)
    up_ref[...] = out_ref[pl.ds(pl.multiple_of((x_ref[0] & 1) * HROWS, HROWS), HROWS)]
    down_ref[...] = out_ref[pl.ds(pl.multiple_of((1 - (x_ref[0] & 1)) * HROWS, HROWS), HROWS)]


def left_stage(x, prods, roots):
    full = pl.BlockSpec(memory_space=pltpu.VMEM)
    return pl.pallas_call(
        left_kernel,
        in_specs=[pl.BlockSpec(memory_space=pltpu.SMEM)] + [full] * (2 * NX),
        out_shape=(
            jax.ShapeDtypeStruct((BS, BS), BF16),
            jax.ShapeDtypeStruct((HROWS, BS), BF16),
            jax.ShapeDtypeStruct((HROWS, BS), BF16),
        ),
        compiler_params=PARAMS,
        cost_estimate=cost(1 << 28, 3 << 19),
    )(x, *prods, *roots)


def place_kernel(spots, x_ref, z_ref, own_ref, *refs):
    srcs, out_ref, sems = refs[:-2], refs[-2], refs[-1]
    halves = {"up": x_ref[0] & 1, "down": 1 - (x_ref[0] & 1)}
    copies = []
    for k, (src, ring, other, quarter, by) in enumerate(zip(srcs, *zip(*spots))):
        half = 0 if ring is None else (1 - halves[ring] if other else halves[ring])
        row = pl.multiple_of(half * HROWS + quarter * QROWS, QROWS)
        col = pl.multiple_of(lax.rem(z_ref[0] + NZ - own_ref[0] + by, NZ) * BS, BS)
        dst = out_ref.at[pl.ds(row, src.shape[0]), pl.ds(col, BS)]
        copies.append(pltpu.make_async_copy(src, dst, sems.at[k]))
        copies[-1].start()
    for copy in copies:
        copy.wait()


def place(x, z, own, pieces):
    srcs, spots = [piece[0] for piece in pieces], [piece[1:] for piece in pieces]
    anywhere = pl.BlockSpec(memory_space=pl.ANY)
    smem = pl.BlockSpec(memory_space=pltpu.SMEM)
    return pl.pallas_call(
        functools.partial(place_kernel, spots),
        in_specs=[smem] * 3 + [pl.BlockSpec(memory_space=pltpu.VMEM)] * len(srcs),
        out_specs=anywhere,
        out_shape=jax.ShapeDtypeStruct((BS, NZ * BS), BF16),
        scratch_shapes=[pltpu.SemaphoreType.DMA((len(pieces),))],
        compiler_params=PARAMS,
        cost_estimate=cost(0, 4 * sum(src.size for src in srcs)),
    )(x, z, own, *srcs)


def shift(value, axis, size, by):
    return lax.ppermute(value, axis, [(k, (k + by) % size) for k in range(size)])


def partner(value, bits):
    return lax.ppermute(value, "x", [(k, k ^ bits) for k in range(NX)])


def mirror(value):
    pairs = [(z * NZ + own, z * NZ + (z - own) % NZ) for z in range(NZ) for own in range(NZ)]
    return lax.ppermute(value, ("z", *OWN), pairs)


def gather_x(value):
    return [value] + [shift(value, "x", NX, by) for by in (1, 3, 2)]


def exchange(value, axis):
    return lax.all_to_all(value, axis, split_axis=0, concat_axis=0, tiled=True)


def after(value, *others):
    return lax.optimization_barrier((value, *others))[0]


def on_device(grads, momentum, second, left_roots, right_roots):
    x, z, own = (lax.axis_index(name).reshape(1) for name in ("x", "z", OWN))
    quarters = grads[0].reshape(NX, QROWS, grads.shape[2])

    steps = (1, 3)
    sends = pick(quarters, x)
    firsts = [partner(sends[h], steps[h]) for h in range(2)]

    low_second = after(second, sends[1])[:, :, 0].astype(BF16)
    states = left_roots[:, 0], momentum[:, :, 0], low_second
    pre, root, *kept = pack(x, z, own, sends[1], quarters, right_roots[:, 0], *states)
    pre = exchange(pre, "z")
    firsts = [after(first, pre) for first in firsts]
    pre, root = mirror(pre), mirror(root)
    roots = gather_x(pre[:, :DROWS].reshape(QROWS, BS))

    seconds = [
        partner(add_quarter(kept[h], firsts[h]), steps[1 - h]) for h in range(2)
    ]
    over_z = exchange(sum_quarter(quarters, firsts, seconds, x, own), "z")
    g_low, prod = right_stage(over_z, pre, after(root, *roots))
    block, up, down = left_stage(x, gather_x(prod), roots)

    pieces = [(block, None, False, 0, 0)]
    g_state = mirror(g_low)
    waits, last = (), (g_state,)
    for step in range(1, NZ // 2):
        up, down = (after(half, *waits) for half in (up, down))
        up, down = shift(up, "z", NZ, 1), shift(down, "z", NZ, NZ - 1)
        others = [partner(up, 1), partner(down, 3)]
        pieces += [
            (up, "up", False, 0, NZ - step),
            (down, "down", False, 0, step),
            (others[0], "up", True, 0, NZ - step),
            (others[1], "down", True, 0, step),
        ]
        waits, last = last, others
    up, down = (after(half, *waits) for half in (up, down))
    up, down = shift(up, "z", NZ, 1), shift(down, "z", NZ, NZ - 1)
    pieces += [(up, "up", False, 0, NZ // 2), (down, "down", False, 0, NZ // 2)]

    g = exchange(after(g_state, *waits).reshape(NZ, DROWS, BS), "z")
    g = in_order(own, g).astype(F32)[:, :, None]
    new_moment, new_second = moments(g, momentum, second)
    return place(x, z, own, pieces), new_moment.astype(BF16), new_second


def solution(mesh):
    named = Mesh(mesh.devices.reshape(NX, NZ, NY, NC), ("x", "z", "y", "core"))
    rep = ("x", "z")
    in_specs = (
        P(rep, OWN, None),
        P(None, rep, OWN, None),
        P(None, rep, OWN, None),
        P(None, OWN, rep, None),
        P(None, OWN, None, None),
    )
    out_specs = (P(OWN, None), P(None, rep, OWN, None), P(None, rep, OWN, None))
    return jax.shard_map(
        on_device, mesh=named, in_specs=in_specs, out_specs=out_specs, check_vma=False
    )
```

```python
import functools

import jax
import jax.numpy as jnp
from jax import lax
from jax.experimental import pallas as pl
from jax.experimental.pallas import tpu as pltpu
from jax.sharding import Mesh, PartitionSpec as P

BETA_ONE = 0.9
BETA_TWO = 0.95
CORRECT_ONE = 1.0 - 0.9**10
CORRECT_TWO = 1.0 - 0.95**10
ADAM_EPS = 1e-08
NORM_EPS = 1e-06

NX, NZ, NY, NC = 4, 8, 4, 2
OWN = ("y", "core")
BS = 512
QROWS = BS // NX
DROWS = QROWS // NZ
HROWS = BS // 2
SUMS = 16
HALF = NZ * BS // 2
VMEM = 40 * 1024 * 1024
PARAMS = pltpu.CompilerParams(vmem_limit_bytes=VMEM)
ALL_VMEM = pltpu.CompilerParams(vmem_limit_bytes=57 * 1024 * 1024)
F32, BF16 = jnp.float32, jnp.bfloat16


def cost(flops, nbytes):
    return pl.CostEstimate(flops=flops, bytes_accessed=nbytes, transcendentals=0)


def moments(g, m, v):
    moment = BETA_ONE * m.astype(F32) + (1.0 - BETA_ONE) * g
    second = BETA_TWO * v.astype(F32) + (1.0 - BETA_TWO) * g * g
    return moment, second


def staged(loads, stores, sems):
    for k, (src, dst) in enumerate(loads):
        pltpu.make_async_copy(src, dst, sems.at[0, k]).start()
    for k, (src, dst) in enumerate(loads):
        pltpu.make_async_copy(src, dst, sems.at[0, k]).wait()
        if k < len(stores):
            pltpu.make_async_copy(*stores[k], sems.at[1, k]).start()
    for k, (src, dst) in enumerate(stores):
        pltpu.make_async_copy(src, dst, sems.at[1, k]).wait()


def pick_kernel(x_ref, src_ref, left_ref, right_ref, hold_ref, sems):
    loads, stores = [], []
    for half, out_ref in enumerate((left_ref, right_ref)):
        for k, bits in enumerate(((1, 2), (3, 2))[half]):
            cols = pl.ds(half * HALF, HALF)
            held = hold_ref.at[2 * half + k]
            loads.append((src_ref.at[x_ref[0] ^ bits, :, cols], held))
            stores.append((held, out_ref.at[k]))
    staged(loads, stores, sems)


def pick(grads, x):
    anywhere = pl.BlockSpec(memory_space=pl.ANY)
    return pl.pallas_call(
        pick_kernel,
        in_specs=[pl.BlockSpec(memory_space=pltpu.SMEM), anywhere],
        out_specs=(anywhere, anywhere),
        out_shape=(jax.ShapeDtypeStruct((2, QROWS, HALF), BF16),) * 2,
        scratch_shapes=[pltpu.VMEM((4, QROWS, HALF), BF16), pltpu.SemaphoreType.DMA((2, 4))],
        compiler_params=ALL_VMEM,
        cost_estimate=cost(0, 4 << 20),
    )(x, grads)


def pack_kernel(x_ref, z_ref, own_ref, grads_ref, right_ref, *refs):
    states, (out_ref, root_ref, left_ref, rest_ref) = refs[:-8], refs[-8:-4]
    hold_ref, hold_root_ref, hold_kept_ref, sems = refs[-4:]
    loads = [
        pltpu.make_async_copy(ref, hold_ref.at[:, pl.ds(k * DROWS, DROWS)], sems.at[0, k])
        for k, ref in enumerate(states)
    ]
    stores = [
        pltpu.make_async_copy(
            hold_ref.at[i], out_ref.at[lax.rem(own_ref[0] + i, NZ)], sems.at[1, i]
        )
        for i in range(NZ)
    ]
    root = right_ref.at[lax.rem(z_ref[0] + NZ - own_ref[0], NZ)]
    others = [(root, hold_root_ref, root_ref)]
    for half, bits, kept_ref in ((0, 3, left_ref), (1, 1, rest_ref)):
        src = grads_ref.at[x_ref[0] ^ bits, :, pl.ds(half * HALF, HALF)]
        others.append((src, hold_kept_ref.at[half], kept_ref))
    more = [
        (
            pltpu.make_async_copy(src, hold, sems.at[0, NZ + k]),
            pltpu.make_async_copy(hold, dst, sems.at[1, NZ + k]),
        )
        for k, (src, hold, dst) in enumerate(others)
    ]
    for copy in loads:
        copy.start()
    for load, _ in more:
        load.start()
    for copy in loads:
        copy.wait()
    for copy in stores:
        copy.start()
    for load, store in more:
        load.wait()
        store.start()
    for copy in stores:
        copy.wait()
    for _, store in more:
        store.wait()


def pack(x, z, own, grads, right, *states):
    anywhere = pl.BlockSpec(memory_space=pl.ANY)
    smem = pl.BlockSpec(memory_space=pltpu.SMEM)
    shapes = [(NZ, len(states) * DROWS, BS), (BS, BS), (QROWS, HALF), (QROWS, HALF)]
    return pl.pallas_call(
        pack_kernel,
        in_specs=[smem] * 3 + [anywhere] * (2 + len(states)),
        out_specs=(anywhere,) * 4,
        out_shape=tuple(jax.ShapeDtypeStruct(shape, BF16) for shape in shapes),
        scratch_shapes=[
            pltpu.VMEM(shapes[0], BF16),
            pltpu.VMEM(shapes[1], BF16),
            pltpu.VMEM((2, QROWS, HALF), BF16),
            pltpu.SemaphoreType.DMA((2, NZ + 3)),
        ],
        compiler_params=pltpu.CompilerParams(vmem_limit_bytes=48 * 1024 * 1024),
        cost_estimate=cost(0, 4 << 20),
    )(x, z, own, grads, right, *states)


def add_kernel(kept_ref, got_ref, out_ref):
    out_ref[...] = (kept_ref[...].astype(F32) + got_ref[0].astype(F32)).astype(BF16)


def add_quarter(kept, got):
    spec = pl.BlockSpec((QROWS, HALF // 2), lambda c: (0, c))
    return pl.pallas_call(
        add_kernel,
        grid=(2,),
        in_specs=[spec, pl.BlockSpec((1, QROWS, HALF // 2), lambda c: (1, 0, c))],
        out_specs=spec,
        out_shape=jax.ShapeDtypeStruct((QROWS, HALF), BF16),
        compiler_params=PARAMS,
        cost_estimate=cost(1 << 19, 3 << 19),
    )(kept, got)


def sum_kernel(x_ref, own_ref, *refs):
    out_ref, j = refs[-1], pl.program_id(0)
    for half in range(2):
        mine_ref, first_ref, second_ref = refs[3 * half : 3 * half + 3]
        total = mine_ref[0].astype(F32) + first_ref[0].astype(F32) + second_ref[...].astype(F32)
        out_ref[lax.rem(own_ref[0] + half * (NZ // 2) + j, NZ)] = total.astype(BF16)


def sum_quarter(grads, firsts, seconds, x, own):
    specs, args = [], []
    for half in range(2):
        specs += [
            pl.BlockSpec((1, QROWS, BS), lambda j, x, own, half=half: (x[0], 0, 4 * half + j)),
            pl.BlockSpec((1, QROWS, BS), lambda j, x, own: (0, 0, j)),
            pl.BlockSpec((QROWS, BS), lambda j, x, own: (0, j)),
        ]
        args += [grads, firsts[half], seconds[half]]
    return pl.pallas_call(
        sum_kernel,
        grid_spec=pltpu.PrefetchScalarGridSpec(
            num_scalar_prefetch=2,
            grid=(NZ // 2,),
            in_specs=specs,
            out_specs=pl.BlockSpec((NZ, QROWS, BS), lambda j, x, own: (0, 0, 0)),
        ),
        out_shape=jax.ShapeDtypeStruct((NZ, QROWS, BS), BF16),
        compiler_params=PARAMS,
        cost_estimate=cost(1 << 20, 4 << 20),
    )(x, own, *args)


def right_kernel(parts_ref, pre_ref, root_ref, low_ref, prod_ref):
    g = parts_ref[0].astype(F32)
    for k in range(1, NZ):
        g += parts_ref[k].astype(F32)
    low = g.astype(BF16)
    low_ref[...] = low
    prod_ref[:QROWS] = jnp.dot(low, root_ref[...], preferred_element_type=F32).astype(BF16)
    m = pre_ref[:, DROWS : 2 * DROWS].reshape(QROWS, BS)
    v = pre_ref[:, 2 * DROWS :].reshape(QROWS, BS)
    moment, second = moments(g, m, v)
    step = moment / CORRECT_ONE / (jnp.sqrt(second / CORRECT_TWO) + ADAM_EPS)
    total = jnp.full((SUMS, BS), jnp.sum(step * step), F32)
    high = total.astype(BF16).astype(F32)
    first = lax.broadcasted_iota(jnp.int32, (SUMS, BS), 0) == 0
    prod_ref[QROWS:] = jnp.where(first, high, total - high).astype(BF16)


def right_stage(parts, pre, root):
    return pl.pallas_call(
        right_kernel,
        out_shape=(
            jax.ShapeDtypeStruct((QROWS, BS), BF16),
            jax.ShapeDtypeStruct((QROWS + SUMS, BS), BF16),
        ),
        compiler_params=PARAMS,
        cost_estimate=cost(1 << 26, 2 << 20),
    )(parts, pre, root)


def order_kernel(own_ref, src_ref, out_ref):
    for k in range(NZ):
        out_ref[lax.rem(k + NZ - own_ref[0], NZ)] = src_ref[k]


def in_order(own, parts):
    full, smem = pl.BlockSpec(memory_space=pltpu.VMEM), pl.BlockSpec(memory_space=pltpu.SMEM)
    return pl.pallas_call(
        order_kernel,
        in_specs=[smem, full],
        out_specs=full,
        out_shape=jax.ShapeDtypeStruct(parts.shape, BF16),
        compiler_params=PARAMS,
        cost_estimate=cost(0, 1 << 18),
    )(own, parts)


def left_kernel(x_ref, *refs):
    prods, roots, (out_ref, up_ref, down_ref) = refs[:NX], refs[NX : 2 * NX], refs[2 * NX :]
    shampoo, adam_sq = None, None
    for prod_ref, root_ref in zip(prods, roots):
        term = lax.dot_general(
            root_ref[...],
            prod_ref[:QROWS],
            (((0,), (0,)), ((), ())),
            preferred_element_type=F32,
        )
        sums = prod_ref[QROWS:].astype(F32)
        part = sums[0:1, 0:1] + sums[1:2, 0:1]
        shampoo = term if shampoo is None else shampoo + term
        adam_sq = part if adam_sq is None else adam_sq + part
    scale = jnp.sqrt((adam_sq + NORM_EPS) / (jnp.sum(shampoo * shampoo) + NORM_EPS))
    out_ref[...] = (shampoo * scale).astype(BF16)
    up_ref[...] = out_ref[pl.ds(pl.multiple_of((x_ref[0] & 1) * HROWS, HROWS), HROWS)]
    down_ref[...] = out_ref[pl.ds(pl.multiple_of((1 - (x_ref[0] & 1)) * HROWS, HROWS), HROWS)]


def left_stage(x, prods, roots):
    full = pl.BlockSpec(memory_space=pltpu.VMEM)
    return pl.pallas_call(
        left_kernel,
        in_specs=[pl.BlockSpec(memory_space=pltpu.SMEM)] + [full] * (2 * NX),
        out_shape=(
            jax.ShapeDtypeStruct((BS, BS), BF16),
            jax.ShapeDtypeStruct((HROWS, BS), BF16),
            jax.ShapeDtypeStruct((HROWS, BS), BF16),
        ),
        compiler_params=PARAMS,
        cost_estimate=cost(1 << 28, 3 << 19),
    )(x, *prods, *roots)


def place_kernel(spots, x_ref, z_ref, own_ref, *refs):
    srcs, out_ref, sems = refs[:-2], refs[-2], refs[-1]
    halves = {"up": x_ref[0] & 1, "down": 1 - (x_ref[0] & 1)}
    copies = []
    for k, (src, ring, other, quarter, by) in enumerate(zip(srcs, *zip(*spots))):
        half = 0 if ring is None else (1 - halves[ring] if other else halves[ring])
        row = pl.multiple_of(half * HROWS + quarter * QROWS, QROWS)
        col = pl.multiple_of(lax.rem(z_ref[0] + NZ - own_ref[0] + by, NZ) * BS, BS)
        dst = out_ref.at[pl.ds(row, src.shape[0]), pl.ds(col, BS)]
        copies.append(pltpu.make_async_copy(src, dst, sems.at[k]))
        copies[-1].start()
    for copy in copies:
        copy.wait()


def place(x, z, own, pieces):
    srcs, spots = [piece[0] for piece in pieces], [piece[1:] for piece in pieces]
    anywhere = pl.BlockSpec(memory_space=pl.ANY)
    smem = pl.BlockSpec(memory_space=pltpu.SMEM)
    return pl.pallas_call(
        functools.partial(place_kernel, spots),
        in_specs=[smem] * 3 + [pl.BlockSpec(memory_space=pltpu.VMEM)] * len(srcs),
        out_specs=anywhere,
        out_shape=jax.ShapeDtypeStruct((BS, NZ * BS), BF16),
        scratch_shapes=[pltpu.SemaphoreType.DMA((len(pieces),))],
        compiler_params=PARAMS,
        cost_estimate=cost(0, 4 * sum(src.size for src in srcs)),
    )(x, z, own, *srcs)


def shift(value, axis, size, by):
    return lax.ppermute(value, axis, [(k, (k + by) % size) for k in range(size)])


def partner(value, bits):
    return lax.ppermute(value, "x", [(k, k ^ bits) for k in range(NX)])


def mirror(value):
    pairs = [(z * NZ + own, z * NZ + (z - own) % NZ) for z in range(NZ) for own in range(NZ)]
    return lax.ppermute(value, ("z", *OWN), pairs)


def gather_x(value):
    return [value] + [shift(value, "x", NX, by) for by in (1, 3, 2)]


def exchange(value, axis):
    return lax.all_to_all(value, axis, split_axis=0, concat_axis=0, tiled=True)


def after(value, *others):
    return lax.optimization_barrier((value, *others))[0]


def on_device(grads, momentum, second, left_roots, right_roots):
    x, z, own = (lax.axis_index(name).reshape(1) for name in ("x", "z", OWN))
    quarters = grads[0].reshape(NX, QROWS, grads.shape[2])

    steps = (1, 3)
    sends = pick(quarters, x)
    firsts = [partner(sends[h], steps[h]) for h in range(2)]

    low_second = after(second, sends[1])[:, :, 0].astype(BF16)
    states = left_roots[:, 0], momentum[:, :, 0], low_second
    pre, root, *kept = pack(x, z, own, quarters, right_roots[:, 0], *states)
    pre = exchange(pre, "z")
    firsts = [after(first, pre) for first in firsts]
    pre, root = mirror(pre), mirror(root)
    roots = gather_x(pre[:, :DROWS].reshape(QROWS, BS))

    seconds = [
        partner(add_quarter(kept[h], firsts[h]), steps[1 - h]) for h in range(2)
    ]
    over_z = exchange(sum_quarter(quarters, firsts, seconds, x, own), "z")
    g_low, prod = right_stage(over_z, pre, after(root, *roots))
    block, up, down = left_stage(x, gather_x(prod), roots)

    pieces = [(block, None, False, 0, 0)]
    g_state = mirror(g_low)
    waits, last = (), (g_state,)
    for step in range(1, NZ // 2):
        up, down = (after(half, *waits) for half in (up, down))
        up, down = shift(up, "z", NZ, 1), shift(down, "z", NZ, NZ - 1)
        others = [partner(up, 1), partner(down, 3)]
        pieces += [
            (up, "up", False, 0, NZ - step),
            (down, "down", False, 0, step),
            (others[0], "up", True, 0, NZ - step),
            (others[1], "down", True, 0, step),
        ]
        waits, last = last, others
    up, down = (after(half, *waits) for half in (up, down))
    up, down = shift(up, "z", NZ, 1), shift(down, "z", NZ, NZ - 1)
    pieces += [(up, "up", False, 0, NZ // 2), (down, "down", False, 0, NZ // 2)]

    g = exchange(after(g_state, *waits).reshape(NZ, DROWS, BS), "z")
    g = in_order(own, g).astype(F32)[:, :, None]
    new_moment, new_second = moments(g, momentum, second)
    return place(x, z, own, pieces), new_moment.astype(BF16), new_second


def solution(mesh):
    named = Mesh(mesh.devices.reshape(NX, NZ, NY, NC), ("x", "z", "y", "core"))
    rep = ("x", "z")
    in_specs = (
        P(rep, OWN, None),
        P(None, rep, OWN, None),
        P(None, rep, OWN, None),
        P(None, OWN, rep, None),
        P(None, OWN, None, None),
    )
    out_specs = (P(OWN, None), P(None, rep, OWN, None), P(None, rep, OWN, None))
    return jax.shard_map(
        on_device, mesh=named, in_specs=in_specs, out_specs=out_specs, check_vma=False
    )
```
